32 devices in a mesh: tensor: 2 (over x), serve: 16 (over z, y, core).
Axes of the slice: x: 2, y: 2, z: 4, core: 2. Of those that a mesh axis runs over, the one named last changes fastest.
Arguments:
- prefill: bfloat16 [32, 1024, 8192], P('serve', None, 'tensor'), may hold values from -6 to 6
- down_proj: bfloat16 [8192, 1024], P('tensor'), may hold values from -0.0625 to 0.0625
- up_key: bfloat16 [512, 1024], P(None, 'tensor'), may hold values from -0.25 to 0.25
- up_value: bfloat16 [512, 1024], P(None, 'tensor'), may hold values from -0.25 to 0.25
- queries: bfloat16 [32, 4, 8192], P('serve', None, 'tensor'), may hold values from -60 to 60
- cache_latent: bfloat16 [32, 1024, 1024], P('serve'), may hold values from -60 to 60
- hist_len: int32 [32], P('serve'), may hold values from 256 to 1024, as said below
- assign: int32 [32], replicated, may hold values from 0 to 31, each once
Outputs:
- attn: bfloat16 [32, 4, 8192], P('serve', None, 'tensor')
- span_latent: bfloat16 [32, 1024, 1024], P('serve', None, 'tensor')
The draws below stay inside these ranges and needn't reach their ends.
Inputs may be any that keep to these rules, and one draw needn't show every extreme that they name: `hist_len`: some slot has exactly 1024 live rows. `assign`: each slot receives exactly one request's span.
All inputs are finite; a program needn't handle non-finite values.
Results may differ from the reference program's by a relative error of at most 0.012.
The reference program's roundings to bfloat16 on the way count: a program that leaves them out, or rounds other values in their place, can miss the bound.
Values may be sent and summed in bfloat16 or wider, within the bound.
A program may use at most 128 MiB of HBM per device.

```python
import jax
import jax.numpy as jnp
from jax import lax

D = 8192
HEADS = 64
KV_HEADS = 8
HEAD_DIM = 128
RANK = 512
SPAN = 1024
STEPS = 4
HIST = 1024
REQS = 32


def draw_queries(key, part):
    key = jax.random.fold_in(key, 23)
    noise_key = jax.random.fold_in(key, 0)
    samples = jax.random.normal(noise_key, (REQS, STEPS, HEADS, HEAD_DIM), jnp.float32)
    samples = jnp.clip(samples * 3.0, -18.0, 18.0)
    return samples.reshape(REQS, STEPS, HEADS * HEAD_DIM).astype(jnp.bfloat16)


def draw_cache_latent(key, part):
    key = jax.random.fold_in(key, 37)
    noise_key = jax.random.fold_in(key, 0)
    samples = jax.random.normal(noise_key, (REQS, HIST, 2 * RANK), jnp.float32)
    samples = jnp.clip(samples, -6.0, 6.0)
    return samples.astype(jnp.bfloat16)


def draw_hist_len(key, part):
    key = jax.random.fold_in(key, 11)
    first_key, second_key = jax.random.split(key)
    lengths = jax.random.randint(first_key, (REQS,), HIST // 4, HIST + 1)
    longest = jax.random.randint(second_key, (), 0, REQS)
    return jnp.where(jnp.arange(REQS) == longest, HIST, lengths).astype(jnp.int32)


def level_of(own_key, extent, cuts, smallest, high):
    def one(axis_at, shards_of):
        heights = jax.random.uniform(jax.random.fold_in(jax.random.fold_in(own_key, 6), axis_at), (shards_of,), jnp.float32, smallest / len(cuts), high / len(cuts))
        return jnp.repeat(jnp.exp(heights), extent[axis_at] // shards_of).reshape((-1,) + (1,) * (len(extent) - axis_at - 1))

    level = one(*cuts[0])
    for cut in cuts[1:]:
        level = level * one(*cut)
    return level


def gaussian(key, shape, deviation, most, shards=(), kind=jnp.bfloat16):
    level = level_of(key, shape, shards, -0.22, 0.18) if shards else 1.0
    entries = jax.random.normal(key, shape, jnp.float32) * deviation * level
    return jnp.minimum(jnp.maximum(entries, -most), most).astype(kind)


def setup_inputs(seed: int = 0) -> dict:
    streams_of = jax.random.split(jax.random.key(seed), 9)
    prefill = gaussian(streams_of[0], (REQS, SPAN, D), 1.0, 6.0, ((0, 16), (2, 2)))
    down_proj = gaussian(streams_of[1], (D, 2 * RANK), D ** -0.5, 0.0625, ((0, 2),))
    up_key = gaussian(streams_of[2], (RANK, KV_HEADS * HEAD_DIM), RANK ** -0.5, 0.25, ((1, 2),))
    up_value = gaussian(streams_of[3], (RANK, KV_HEADS * HEAD_DIM), RANK ** -0.5, 0.25, ((1, 2),))
    queries = draw_queries(jax.random.fold_in(streams_of[8], 71), 0)
    cache_latent = draw_cache_latent(jax.random.fold_in(streams_of[8], 71), 0)
    hist_len = draw_hist_len(jax.random.fold_in(streams_of[8], 71), 0)
    assign = jax.random.permutation(streams_of[7], REQS).astype(jnp.int32)
    return {"prefill": prefill, "down_proj": down_proj, "up_key": up_key, "up_value": up_value, "queries": queries, "cache_latent": cache_latent, "hist_len": hist_len, "assign": assign}


ROPE_BASE = 500000.0


def rotate(vectors, positions):
    half = vectors.shape[-1] // 2
    frequency = ROPE_BASE ** (-jnp.arange(half, dtype=jnp.float32) / half)
    angles = positions.astype(jnp.float32)[..., None, None] * frequency
    cosine = jnp.cos(angles)
    sine = jnp.sin(angles)
    first_half = vectors[..., :half]
    second_half = vectors[..., half:]
    return jnp.concatenate([first_half * cosine - second_half * sine, second_half * cosine + first_half * sine], axis=-1)


def reference(prefill, down_proj, up_key, up_value, queries, cache_latent, hist_len, assign):
    source_of = jnp.zeros((REQS,), jnp.int32).at[assign].set(jnp.arange(REQS, dtype=jnp.int32))
    group_size = HEADS // KV_HEADS
    score_scale = HEAD_DIM ** -0.5

    def one_slot(operands):
        cache_rows, source, history, query_rows = operands
        span_rows = jnp.dot(prefill[source], down_proj, preferred_element_type=jnp.float32).astype(jnp.bfloat16)
        all_rows = jnp.concatenate([cache_rows, span_rows], axis=0)
        positions = jnp.concatenate([jnp.arange(HIST, dtype=jnp.int32), history + jnp.arange(SPAN, dtype=jnp.int32)])
        keys = jnp.dot(all_rows[:, :RANK], up_key, preferred_element_type=jnp.float32).reshape(HIST + SPAN, KV_HEADS, HEAD_DIM)
        keys = rotate(keys, positions).astype(jnp.bfloat16)
        values = jnp.dot(all_rows[:, RANK:], up_value, preferred_element_type=jnp.float32).astype(jnp.bfloat16)
        values = values.reshape(HIST + SPAN, KV_HEADS, HEAD_DIM)
        query_pos = history + SPAN + jnp.arange(STEPS, dtype=jnp.int32)
        rotated = rotate(query_rows.astype(jnp.float32).reshape(STEPS, HEADS, HEAD_DIM), query_pos).astype(jnp.bfloat16)
        rotated = rotated.reshape(STEPS, KV_HEADS, group_size, HEAD_DIM)
        scores = jnp.einsum("skgd,nkd->skgn", rotated.astype(jnp.float32), keys.astype(jnp.float32)) * score_scale
        row_index = jnp.arange(HIST + SPAN, dtype=jnp.int32)
        live = (row_index < history) | (row_index >= HIST)
        scores = jnp.where(live, scores, -jnp.inf)
        highest = jnp.max(scores, axis=-1, keepdims=True)
        weights = jnp.exp(scores - highest)
        probs = (weights / jnp.sum(weights, axis=-1, keepdims=True)).astype(jnp.bfloat16)
        mixed = jnp.einsum("skgn,nkd->skgd", probs.astype(jnp.float32), values.astype(jnp.float32))
        return mixed.reshape(STEPS, HEADS * HEAD_DIM).astype(jnp.bfloat16), span_rows

    attn, span_latent = lax.map(one_slot, (cache_latent, source_of, hist_len, queries))
    return attn, span_latent
```

```python
import functools

import jax
import jax.numpy as jnp
from jax import lax
from jax.experimental import pallas as pl
from jax.experimental.pallas import tpu as pltpu
from jax.sharding import PartitionSpec as P

HEAD_DIM = 128


ROPE_BASE = 500000.0


def rotate(vectors, positions):
    half = vectors.shape[-1] // 2
    frequency = ROPE_BASE ** (-jnp.arange(half, dtype=jnp.float32) / half)
    angles = positions.astype(jnp.float32)[..., None, None] * frequency
    cosine = jnp.cos(angles)
    sine = jnp.sin(angles)
    first_half = vectors[..., :half]
    second_half = vectors[..., half:]
    return jnp.concatenate(
        [first_half * cosine - second_half * sine, second_half * cosine + first_half * sine],
        axis=-1,
    )


MESH = pl.DeviceIdType.MESH
LAG = 2


def hand_off_kernel(
    prefill_ref,
    down_ref,
    source_ref,
    mine_out,
    other_out,
    tokens,
    partial,
    arrived_partial,
    own,
    piece,
    spread,
    staged,
    mine,
    other,
    load_sem,
    partial_send,
    partial_recv,
    spread_send,
    spread_recv,
    home_send,
    home_recv,
    share_send,
    share_recv,
    store_sem,
):
    serve_count, slot_count, rows, width = piece.shape
    tensor = lax.axis_index("tensor")
    serve = lax.axis_index("serve")
    peer = 1 - tensor

    barrier = pltpu.get_barrier_semaphore()
    pl.semaphore_signal(barrier, inc=1, device_id={"tensor": peer}, device_id_type=MESH)

    @pl.loop(1, serve_count)
    def _(step):
        pl.semaphore_signal(
            barrier,
            inc=1,
            device_id={"serve": lax.rem(serve + step, serve_count)},
            device_id_type=MESH,
        )

    def target(step):
        return lax.rem(serve + step + 1, serve_count)

    def origin(step):
        return lax.rem(serve + 2 * serve_count - step - 1, serve_count)

    def load(step):
        start = pl.multiple_of(target(step) * rows, rows)
        return pltpu.make_async_copy(
            prefill_ref.at[:, pl.ds(start, rows), :],
            tokens.at[lax.rem(step, 2)],
            load_sem.at[lax.rem(step, 2)],
        )

    def partial_copy(step):
        return pltpu.make_async_remote_copy(
            src_ref=partial.at[step],
            dst_ref=arrived_partial.at[step],
            send_sem=partial_send.at[step],
            recv_sem=partial_recv.at[step],
            device_id={"tensor": peer},
            device_id_type=MESH,
        )

    def spread_copy(step, place):
        return pltpu.make_async_remote_copy(
            src_ref=piece.at[step],
            dst_ref=spread.at[place],
            send_sem=spread_send.at[step],
            recv_sem=spread_recv.at[place],
            device_id={"serve": target(step)},
            device_id_type=MESH,
        )

    def home_copy(step, place):
        start = pl.multiple_of(place * rows, rows)
        return pltpu.make_async_remote_copy(
            src_ref=staged.at[step],
            dst_ref=mine.at[:, pl.ds(start, rows), :],
            send_sem=home_send.at[step],
            recv_sem=home_recv.at[place],
            device_id={"serve": target(step)},
            device_id_type=MESH,
        )

    def share_copy(place):
        start = pl.multiple_of(place * rows, rows)
        return pltpu.make_async_remote_copy(
            src_ref=mine.at[:, pl.ds(start, rows), :],
            dst_ref=other.at[:, pl.ds(start, rows), :],
            send_sem=share_send.at[place],
            recv_sem=share_recv.at[place],
            device_id={"tensor": peer},
            device_id_type=MESH,
        )

    load(0).start()
    pl.semaphore_wait(barrier, serve_count)
    peer_columns = pl.ds(pl.multiple_of(peer * width, width), width)
    own_columns = pl.ds(pl.multiple_of(tensor * width, width), width)

    def project(step):
        load(step).wait()

        @pl.when(step + 1 < serve_count)
        def _():
            load(step + 1).start()

        block = tokens[lax.rem(step, 2)].reshape(slot_count * rows, -1)
        partial[step] = jnp.dot(
            block, down_ref[:, peer_columns], preferred_element_type=jnp.float32
        ).astype(jnp.bfloat16)
        partial_copy(step).start()
        own[step] = jnp.dot(block, down_ref[:, own_columns], preferred_element_type=jnp.float32)

    def finish(step):
        partial_copy(step).wait_recv()
        latent = (own[step] + arrived_partial[step].astype(jnp.float32)).astype(jnp.bfloat16)
        latent = latent.reshape(slot_count, rows, width)

        @pl.when(step < serve_count - 1)
        def _():
            piece[step] = latent
            spread_copy(step, serve).start()

        @pl.when(step == serve_count - 1)
        def _():
            spread[serve] = latent

    @pl.loop(0, serve_count)
    def _(step):
        project(step)

        @pl.when(step >= LAG)
        def _():
            finish(step - LAG)

    @pl.loop(serve_count - LAG, serve_count)
    def _(step):
        finish(step)

    @pl.loop(0, serve_count - 1)
    def _(step):
        spread_copy(step, origin(step)).wait_recv()

    @pl.loop(0, serve_count)
    def _(step):
        for index in range(slot_count):
            source = source_ref[target(step) * slot_count + index]
            staged[step, index] = spread[source // slot_count, lax.rem(source, slot_count)]

        @pl.when(step < serve_count - 1)
        def _():
            home_copy(step, serve).start()

        @pl.when(step == serve_count - 1)
        def _():
            start = pl.multiple_of(serve * rows, rows)
            mine[:, pl.ds(start, rows), :] = staged[step]
            share_copy(serve).start()

    @pl.loop(0, serve_count - 1)
    def _(step):
        place = origin(step)
        home_copy(step, place).wait_recv()
        share_copy(place).start()

    mine_store = pltpu.make_async_copy(mine, mine_out, store_sem.at[0])
    mine_store.start()

    @pl.loop(0, serve_count)
    def _(step):
        share_copy(step).wait()
        partial_copy(step).wait_send()

        @pl.when(step < serve_count - 1)
        def _():
            spread_copy(step, serve).wait_send()
            home_copy(step, serve).wait_send()

    other_store = pltpu.make_async_copy(other, other_out, store_sem.at[1])
    other_store.start()
    other_store.wait()
    mine_store.wait()


def hand_off(prefill, down_proj, source_of):
    slot_count, span_count, feature_count = prefill.shape
    serve_count = lax.axis_size("serve")
    width = down_proj.shape[1] // lax.axis_size("tensor")
    rows = span_count // serve_count
    half = jax.ShapeDtypeStruct((slot_count, span_count, width), jnp.bfloat16)
    pieces = (serve_count, slot_count, rows, width)
    flat = (serve_count, slot_count * rows, width)
    each = pltpu.SemaphoreType.DMA((serve_count,))
    return pl.pallas_call(
        hand_off_kernel,
        out_shape=(half, half),
        in_specs=[
            pl.BlockSpec(memory_space=pl.ANY),
            pl.BlockSpec(memory_space=pltpu.VMEM),
            pl.BlockSpec(memory_space=pltpu.SMEM),
        ],
        out_specs=(pl.BlockSpec(memory_space=pl.ANY), pl.BlockSpec(memory_space=pl.ANY)),
        scratch_shapes=[
            pltpu.VMEM((2, slot_count, rows, feature_count), jnp.bfloat16),
            pltpu.VMEM(flat, jnp.bfloat16),
            pltpu.VMEM(flat, jnp.bfloat16),
            pltpu.VMEM(flat, jnp.float32),
            pltpu.VMEM(pieces, jnp.bfloat16),
            pltpu.VMEM(pieces, jnp.bfloat16),
            pltpu.VMEM(pieces, jnp.bfloat16),
            pltpu.VMEM(half.shape, jnp.bfloat16),
            pltpu.VMEM(half.shape, jnp.bfloat16),
            pltpu.SemaphoreType.DMA((2,)),
            each,
            each,
            each,
            each,
            each,
            each,
            each,
            each,
            pltpu.SemaphoreType.DMA((2,)),
        ],
        compiler_params=pltpu.CompilerParams(
            collective_id=0, has_side_effects=True, vmem_limit_bytes=56 * 2**20
        ),
        cost_estimate=pl.CostEstimate(
            flops=4 * slot_count * span_count * feature_count * width,
            bytes_accessed=2 * slot_count * span_count * feature_count,
            transcendentals=0,
        ),
    )(prefill, down_proj, source_of)


def shards(prefill, down_proj, up_key, up_value, queries, cache_latent, hist_len, assign):
    slot_count, span_count, _ = prefill.shape
    rank_width = down_proj.shape[1] // 2
    request = jnp.arange(assign.shape[0], dtype=jnp.int32)
    source_of = jnp.sum(jnp.where(assign[None, :] == request[:, None], request[None, :], 0), axis=1)
    span_out, other = hand_off(prefill, down_proj, source_of)
    first = lax.axis_index("tensor") == 0
    key_latent = jnp.where(first, span_out, other)
    value_latent = jnp.where(first, other, span_out)
    kv_local = up_key.shape[1] // HEAD_DIM
    head_local = queries.shape[2] // HEAD_DIM
    group_size = head_local // kv_local
    history = cache_latent.shape[1]
    step_count = queries.shape[1]
    score_scale = HEAD_DIM ** (-0.5)
    cache_keys = jnp.dot(cache_latent[..., :rank_width], up_key, preferred_element_type=jnp.float32)
    cache_keys = cache_keys.reshape(slot_count, history, kv_local, HEAD_DIM)
    cache_pos = jnp.broadcast_to(
        jnp.arange(history, dtype=jnp.int32)[None, :], (slot_count, history)
    )
    cache_keys = rotate(cache_keys, cache_pos).astype(jnp.bfloat16)
    cache_values = jnp.dot(
        cache_latent[..., rank_width:], up_value, preferred_element_type=jnp.float32
    ).astype(jnp.bfloat16)
    cache_values = cache_values.reshape(slot_count, history, kv_local, HEAD_DIM)
    span_keys = jnp.dot(key_latent, up_key, preferred_element_type=jnp.float32)
    span_keys = span_keys.reshape(slot_count, span_count, kv_local, HEAD_DIM)
    span_pos = hist_len[:, None] + jnp.arange(span_count, dtype=jnp.int32)[None, :]
    span_keys = rotate(span_keys, span_pos).astype(jnp.bfloat16)
    span_values = jnp.dot(
        value_latent, up_value, preferred_element_type=jnp.float32
    ).astype(jnp.bfloat16)
    span_values = span_values.reshape(slot_count, span_count, kv_local, HEAD_DIM)
    query_pos = hist_len[:, None] + span_count + jnp.arange(step_count, dtype=jnp.int32)[None, :]
    rotated = rotate(
        queries.astype(jnp.float32).reshape(slot_count, step_count, head_local, HEAD_DIM), query_pos
    ).astype(jnp.bfloat16)
    rotated = rotated.reshape(slot_count, step_count, kv_local, group_size, HEAD_DIM)
    cache_scores = (
        jnp.einsum("cskgd,cnkd->cskgn", rotated, cache_keys, preferred_element_type=jnp.float32)
        * score_scale
    )
    live = jnp.arange(history, dtype=jnp.int32)[None, :] < hist_len[:, None]
    cache_scores = jnp.where(live[:, None, None, None, :], cache_scores, -jnp.inf)
    span_scores = (
        jnp.einsum("cskgd,cmkd->cskgm", rotated, span_keys, preferred_element_type=jnp.float32)
        * score_scale
    )
    highest = jnp.maximum(jnp.max(cache_scores, axis=-1), jnp.max(span_scores, axis=-1))
    cache_weights = jnp.exp(cache_scores - highest[..., None])
    span_weights = jnp.exp(span_scores - highest[..., None])
    totals = jnp.sum(cache_weights, axis=-1) + jnp.sum(span_weights, axis=-1)
    cache_probs = (cache_weights / totals[..., None]).astype(jnp.bfloat16)
    span_probs = (span_weights / totals[..., None]).astype(jnp.bfloat16)
    mixed = jnp.einsum(
        "cskgn,cnkd->cskgd", cache_probs, cache_values, preferred_element_type=jnp.float32
    )
    mixed = mixed + jnp.einsum(
        "cskgm,cmkd->cskgd", span_probs, span_values, preferred_element_type=jnp.float32
    )
    attn = mixed.astype(jnp.bfloat16).reshape(slot_count, step_count, head_local * HEAD_DIM)
    return (attn, span_out)


def solution(mesh):
    return jax.shard_map(
        shards,
        mesh=mesh,
        in_specs=(
            P("serve", None, "tensor"),
            P("tensor", None),
            P(None, "tensor"),
            P(None, "tensor"),
            P("serve", None, "tensor"),
            P("serve", None, None),
            P("serve"),
            P(),
        ),
        out_specs=(P("serve", None, "tensor"), P("serve", None, "tensor")),
        check_vma=False,
    )
```

```python
import jax
import jax.numpy as jnp
import numpy as np
from jax import lax
from jax.experimental import pallas as pl
from jax.experimental.pallas import tpu as pltpu
from jax.sharding import PartitionSpec as P

HEAD_DIM = 128


ROPE_BASE = 500000.0


def rotate(vectors, positions):
    half = vectors.shape[-1] // 2
    frequency = ROPE_BASE ** (-jnp.arange(half, dtype=jnp.float32) / half)
    angles = positions.astype(jnp.float32)[..., None, None] * frequency
    cosine = jnp.cos(angles)
    sine = jnp.sin(angles)
    first_half = vectors[..., :half]
    second_half = vectors[..., half:]
    return jnp.concatenate(
        [first_half * cosine - second_half * sine, second_half * cosine + first_half * sine],
        axis=-1,
    )


MESH = pl.DeviceIdType.MESH
LAG = 2


def hand_off_kernel(
    prefill_ref,
    down_ref,
    source_ref,
    length_ref,
    query_ref,
    turn_ref,
    cosine_ref,
    sine_ref,
    up_key_ref,
    up_value_ref,
    cache_ref,
    span_out,
    attn_ref,
    tokens,
    partial,
    arrived_partial,
    own,
    piece,
    spread,
    staged,
    latents,
    cached,
    keys,
    values,
    scores,
    load_sem,
    partial_send,
    partial_recv,
    spread_send,
    spread_recv,
    home_send,
    home_recv,
    share_send,
    share_recv,
    store_sem,
    cache_sem,
):
    serve_count, slot_count, rows, width = piece.shape
    tensor = lax.axis_index("tensor")
    serve = lax.axis_index("serve")
    peer = 1 - tensor

    barrier = pltpu.get_barrier_semaphore()
    pl.semaphore_signal(barrier, inc=1, device_id={"tensor": peer}, device_id_type=MESH)

    @pl.loop(1, serve_count)
    def _(step):
        pl.semaphore_signal(
            barrier,
            inc=1,
            device_id={"serve": lax.rem(serve + step, serve_count)},
            device_id_type=MESH,
        )

    def target(step):
        return lax.rem(serve + step + 1, serve_count)

    def origin(step):
        return lax.rem(serve + 2 * serve_count - step - 1, serve_count)

    def load(step):
        start = pl.multiple_of(target(step) * rows, rows)
        return pltpu.make_async_copy(
            prefill_ref.at[:, pl.ds(start, rows), :],
            tokens.at[lax.rem(step, 2)],
            load_sem.at[lax.rem(step, 2)],
        )

    def partial_copy(step):
        return pltpu.make_async_remote_copy(
            src_ref=partial.at[step],
            dst_ref=arrived_partial.at[step],
            send_sem=partial_send.at[step],
            recv_sem=partial_recv.at[step],
            device_id={"tensor": peer},
            device_id_type=MESH,
        )

    def spread_copy(step, place):
        return pltpu.make_async_remote_copy(
            src_ref=piece.at[step],
            dst_ref=spread.at[place],
            send_sem=spread_send.at[step],
            recv_sem=spread_recv.at[place],
            device_id={"serve": target(step)},
            device_id_type=MESH,
        )

    def home_copy(step, place):
        start = pl.multiple_of(place * rows, rows)
        return pltpu.make_async_remote_copy(
            src_ref=staged.at[step],
            dst_ref=latents.at[tensor, :, pl.ds(start, rows), :],
            send_sem=home_send.at[step],
            recv_sem=home_recv.at[place],
            device_id={"serve": target(step)},
            device_id_type=MESH,
        )

    def share_copy(place):
        start = pl.multiple_of(place * rows, rows)
        return pltpu.make_async_remote_copy(
            src_ref=latents.at[tensor, :, pl.ds(start, rows), :],
            dst_ref=latents.at[tensor, :, pl.ds(start, rows), :],
            send_sem=share_send.at[place],
            recv_sem=share_recv.at[place],
            device_id={"tensor": peer},
            device_id_type=MESH,
        )

    history = cached.shape[1]
    kv_count = query_ref.shape[1]
    score_scale = HEAD_DIM ** (-0.5)

    def write_keys(key_rows, value_rows, cosines, sines, place):
        key_block = jnp.dot(
            key_rows.reshape(slot_count * rows, width),
            up_key_ref[...],
            preferred_element_type=jnp.float32,
        )
        value_block = jnp.dot(
            value_rows.reshape(slot_count * rows, width),
            up_value_ref[...],
            preferred_element_type=jnp.float32,
        ).astype(jnp.bfloat16)
        for index in range(slot_count):
            values[index, pl.ds(place, rows), :] = value_block[index * rows : (index + 1) * rows]
            for head in range(kv_count):
                block = key_block[
                    index * rows : (index + 1) * rows, head * HEAD_DIM : (head + 1) * HEAD_DIM
                ]
                turned = pltpu.roll(block, HEAD_DIM // 2, 1)
                keys[index, pl.ds(place, rows), head * HEAD_DIM : (head + 1) * HEAD_DIM] = (
                    block * cosines[index] + turned * sines[index]
                ).astype(jnp.bfloat16)

    def cache_rows(step):
        place = pl.multiple_of(step * rows, rows)
        block = cached[:, pl.ds(place, rows), :]
        cosine = cosine_ref[pl.ds(place, rows), :]
        sine = sine_ref[pl.ds(place, rows), :]
        write_keys(
            block[..., :width], block[..., width:], [cosine] * slot_count, [sine] * slot_count, place
        )

    def span_rows(place):
        start = pl.multiple_of(place * rows, rows)
        cosine = cosine_ref[pl.ds(start, rows), :]
        sine = sine_ref[pl.ds(start, rows), :]
        cosines = []
        sines = []
        for index in range(slot_count):
            turn_cosine = turn_ref[0, index : index + 1, :]
            turn_sine = turn_ref[1, index : index + 1, :]
            cosines.append(turn_cosine * cosine - turn_sine * sine)
            sines.append(turn_sine * cosine + turn_cosine * sine)
        block = latents[:, :, pl.ds(start, rows), :]
        write_keys(block[0], block[1], cosines, sines, pl.multiple_of(history + start, rows))

    def score(index, head, first, count):
        block = keys[index, first : first + count, head * HEAD_DIM : (head + 1) * HEAD_DIM]
        return (
            lax.dot_general(
                query_ref[index, head],
                block,
                (((1,), (1,)), ((), ())),
                preferred_element_type=jnp.float32,
            )
            * score_scale
        )

    cache_load = pltpu.make_async_copy(cache_ref, cached, cache_sem.at[0])
    cache_load.start()
    load(0).start()
    pl.semaphore_wait(barrier, serve_count)
    peer_columns = pl.ds(pl.multiple_of(peer * width, width), width)
    own_columns = pl.ds(pl.multiple_of(tensor * width, width), width)

    def project(step):
        load(step).wait()

        @pl.when(step + 1 < serve_count)
        def _():
            load(step + 1).start()

        block = tokens[lax.rem(step, 2)].reshape(slot_count * rows, -1)
        partial[step] = jnp.dot(
            block, down_ref[:, peer_columns], preferred_element_type=jnp.float32
        ).astype(jnp.bfloat16)
        partial_copy(step).start()
        own[step] = jnp.dot(block, down_ref[:, own_columns], preferred_element_type=jnp.float32)

    def finish(step):
        partial_copy(step).wait_recv()
        latent = (own[step] + arrived_partial[step].astype(jnp.float32)).astype(jnp.bfloat16)
        latent = latent.reshape(slot_count, rows, width)

        @pl.when(step < serve_count - 1)
        def _():
            piece[step] = latent
            spread_copy(step, serve).start()

        @pl.when(step == serve_count - 1)
        def _():
            spread[serve] = latent

    cache_load.wait()

    @pl.loop(0, serve_count)
    def _(step):
        project(step)
        cache_rows(step)

        @pl.when(step >= LAG)
        def _():
            finish(step - LAG)

    @pl.loop(serve_count - LAG, serve_count)
    def _(step):
        finish(step)

    @pl.loop(0, serve_count - 1)
    def _(step):
        spread_copy(step, origin(step)).wait_recv()

    @pl.loop(0, serve_count)
    def _(step):
        for index in range(slot_count):
            source = source_ref[target(step) * slot_count + index]
            staged[step, index] = spread[source // slot_count, lax.rem(source, slot_count)]

        @pl.when(step < serve_count - 1)
        def _():
            home_copy(step, serve).start()

        @pl.when(step == serve_count - 1)
        def _():
            start = pl.multiple_of(serve * rows, rows)
            latents[tensor, :, pl.ds(start, rows), :] = staged[step]
            share_copy(serve).start()

    for index in range(slot_count):
        row = lax.broadcasted_iota(jnp.int32, (query_ref.shape[2], history), 1)
        live = row < length_ref[index]
        for head in range(kv_count):
            scores[index, head, :, :history] = jnp.where(
                live, score(index, head, 0, history), -jnp.inf
            )

    def take(step):
        place = origin(step)
        share_copy(place).wait_recv()
        span_rows(place)

    @pl.loop(0, serve_count - 1)
    def _(step):
        place = origin(step)
        home_copy(step, place).wait_recv()
        share_copy(place).start()

        @pl.when(step >= LAG)
        def _():
            take(step - LAG)

    span_store = pltpu.make_async_copy(latents.at[tensor], span_out, store_sem.at[0])
    span_store.start()

    @pl.loop(serve_count - 1 - LAG, serve_count)
    def _(step):
        take(step)

    span_count = latents.shape[2]
    for index in range(slot_count):
        for head in range(kv_count):
            cache_scores = scores[index, head, :, :history]
            span_scores = score(index, head, history, span_count)
            highest = jnp.maximum(
                jnp.max(cache_scores, axis=-1, keepdims=True),
                jnp.max(span_scores, axis=-1, keepdims=True),
            )
            cache_weights = jnp.exp(cache_scores - highest)
            span_weights = jnp.exp(span_scores - highest)
            total = jnp.sum(cache_weights, axis=-1, keepdims=True) + jnp.sum(
                span_weights, axis=-1, keepdims=True
            )
            columns = slice(head * HEAD_DIM, (head + 1) * HEAD_DIM)
            mixed = jnp.dot(
                (cache_weights / total).astype(jnp.bfloat16),
                values[index, :history, columns],
                preferred_element_type=jnp.float32,
            ) + jnp.dot(
                (span_weights / total).astype(jnp.bfloat16),
                values[index, history:, columns],
                preferred_element_type=jnp.float32,
            )
            attn_ref[index, head] = mixed.astype(jnp.bfloat16)

    @pl.loop(0, serve_count)
    def _(step):
        share_copy(step).wait_send()
        partial_copy(step).wait_send()

        @pl.when(step < serve_count - 1)
        def _():
            spread_copy(step, serve).wait_send()
            home_copy(step, serve).wait_send()

    span_store.wait()


def tables(count):
    frequency = ROPE_BASE ** (-np.arange(HEAD_DIM // 2) / (HEAD_DIM // 2))
    angles = np.arange(count)[:, None] * frequency
    cosine = np.cos(angles)
    sine = np.sin(angles)
    return (
        jnp.asarray(np.concatenate([cosine, cosine], axis=1), jnp.float32),
        jnp.asarray(np.concatenate([-sine, sine], axis=1), jnp.float32),
    )


def hand_off(
    prefill, down_proj, source_of, hist_len, rotated, turn, up_key, up_value, cache_latent
):
    slot_count, span_count, feature_count = prefill.shape
    serve_count = lax.axis_size("serve")
    width = down_proj.shape[1] // lax.axis_size("tensor")
    rows = span_count // serve_count
    half = jax.ShapeDtypeStruct((slot_count, span_count, width), jnp.bfloat16)
    pieces = (serve_count, slot_count, rows, width)
    flat = (serve_count, slot_count * rows, width)
    history = cache_latent.shape[1]
    cosine, sine = tables(max(history, span_count))
    vmem = pl.BlockSpec(memory_space=pltpu.VMEM)
    smem = pl.BlockSpec(memory_space=pltpu.SMEM)
    hbm = pl.BlockSpec(memory_space=pl.ANY)
    each = pltpu.SemaphoreType.DMA((serve_count,))
    return pl.pallas_call(
        hand_off_kernel,
        out_shape=(half, jax.ShapeDtypeStruct(rotated.shape, jnp.bfloat16)),
        in_specs=[hbm, vmem, smem, smem, vmem, vmem, vmem, vmem, vmem, vmem, hbm],
        out_specs=(hbm, vmem),
        scratch_shapes=[
            pltpu.VMEM((2, slot_count, rows, feature_count), jnp.bfloat16),
            pltpu.VMEM(flat, jnp.bfloat16),
            pltpu.VMEM(flat, jnp.bfloat16),
            pltpu.VMEM(flat, jnp.float32),
            pltpu.VMEM(pieces, jnp.bfloat16),
            pltpu.VMEM(pieces, jnp.bfloat16),
            pltpu.VMEM(pieces, jnp.bfloat16),
            pltpu.VMEM((2,) + half.shape, jnp.bfloat16),
            pltpu.VMEM(cache_latent.shape, jnp.bfloat16),
            pltpu.VMEM((slot_count, history + span_count, up_key.shape[1]), jnp.bfloat16),
            pltpu.VMEM((slot_count, history + span_count, up_key.shape[1]), jnp.bfloat16),
            pltpu.VMEM(rotated.shape[:3] + (history,), jnp.float32),
            pltpu.SemaphoreType.DMA((2,)),
            each,
            each,
            each,
            each,
            each,
            each,
            each,
            each,
            pltpu.SemaphoreType.DMA((1,)),
            pltpu.SemaphoreType.DMA((1,)),
        ],
        compiler_params=pltpu.CompilerParams(
            collective_id=0, has_side_effects=True, vmem_limit_bytes=56 * 2**20
        ),
        cost_estimate=pl.CostEstimate(
            flops=4 * slot_count * span_count * feature_count * width,
            bytes_accessed=2 * slot_count * span_count * feature_count,
            transcendentals=0,
        ),
    )(
        prefill,
        down_proj,
        source_of,
        hist_len,
        rotated,
        turn,
        cosine,
        sine,
        up_key,
        up_value,
        cache_latent,
    )


def shards(prefill, down_proj, up_key, up_value, queries, cache_latent, hist_len, assign):
    slot_count, span_count, _ = prefill.shape
    rank_width = down_proj.shape[1] // 2
    request = jnp.arange(assign.shape[0], dtype=jnp.int32)
    source_of = jnp.sum(jnp.where(assign[None, :] == request[:, None], request[None, :], 0), axis=1)
    kv_local = up_key.shape[1] // HEAD_DIM
    head_local = queries.shape[2] // HEAD_DIM
    group_size = head_local // kv_local
    step_count = queries.shape[1]
    query_pos = hist_len[:, None] + span_count + jnp.arange(step_count, dtype=jnp.int32)[None, :]
    rotated = rotate(
        queries.astype(jnp.float32).reshape(slot_count, step_count, head_local, HEAD_DIM), query_pos
    ).astype(jnp.bfloat16)
    rotated = jnp.swapaxes(
        rotated.reshape(slot_count, step_count, kv_local, group_size, HEAD_DIM), 1, 2
    ).reshape(slot_count, kv_local, step_count * group_size, HEAD_DIM)
    half = HEAD_DIM // 2
    frequency = ROPE_BASE ** (-jnp.arange(half, dtype=jnp.float32) / half)
    angles = hist_len.astype(jnp.float32)[:, None] * frequency
    cosine = jnp.cos(angles)
    sine = jnp.sin(angles)
    turn = jnp.stack(
        [jnp.concatenate([cosine, cosine], axis=1), jnp.concatenate([-sine, sine], axis=1)]
    )
    span_out, attn = hand_off(
        prefill, down_proj, source_of, hist_len, rotated, turn, up_key, up_value, cache_latent
    )
    attn = jnp.swapaxes(
        attn.reshape(slot_count, kv_local, step_count, group_size, HEAD_DIM), 1, 2
    ).reshape(slot_count, step_count, head_local * HEAD_DIM)
    return (attn, span_out)


def solution(mesh):
    return jax.shard_map(
        shards,
        mesh=mesh,
        in_specs=(
            P("serve", None, "tensor"),
            P("tensor", None),
            P(None, "tensor"),
            P(None, "tensor"),
            P("serve", None, "tensor"),
            P("serve", None, None),
            P("serve"),
            P(),
        ),
        out_specs=(P("serve", None, "tensor"), P("serve", None, "tensor")),
        check_vma=False,
    )
```

```python
import jax
import jax.numpy as jnp
import numpy as np
from jax import lax
from jax.experimental import pallas as pl
from jax.experimental.pallas import tpu as pltpu
from jax.sharding import PartitionSpec as P

HEAD_DIM = 128


ROPE_BASE = 500000.0


def rotate(vectors, positions):
    half = vectors.shape[-1] // 2
    frequency = ROPE_BASE ** (-jnp.arange(half, dtype=jnp.float32) / half)
    angles = positions.astype(jnp.float32)[..., None, None] * frequency
    cosine = jnp.cos(angles)
    sine = jnp.sin(angles)
    first_half = vectors[..., :half]
    second_half = vectors[..., half:]
    return jnp.concatenate(
        [first_half * cosine - second_half * sine, second_half * cosine + first_half * sine],
        axis=-1,
    )


MESH = pl.DeviceIdType.MESH
MATMUL_ROWS = 256
LEAST_ROWS = 16


def hand_off_kernel(
    prefill_ref,
    down_ref,
    source_ref,
    length_ref,
    query_ref,
    turn_ref,
    cosine_ref,
    sine_ref,
    up_key_ref,
    up_value_ref,
    cache_ref,
    span_out,
    attn_ref,
    tokens,
    partial,
    arrived_partial,
    own,
    piece,
    spread,
    staged,
    latents,
    cached,
    keys,
    values,
    scores,
    load_sem,
    partial_send,
    partial_recv,
    spread_send,
    spread_recv,
    home_send,
    home_recv,
    share_send,
    share_recv,
    store_sem,
    cache_sem,
):
    group_count = len(spread)
    serve_count, slot_count, rows, width = spread[0].shape
    piece_count = group_count * serve_count
    batch = tokens.shape[1]
    batch_count = piece_count // batch
    group_batches = serve_count // batch
    tensor = lax.axis_index("tensor")
    serve = lax.axis_index("serve")
    peer = 1 - tensor

    barrier = pltpu.get_barrier_semaphore()
    pl.semaphore_signal(barrier, inc=1, device_id={"tensor": peer}, device_id_type=MESH)

    @pl.loop(1, serve_count)
    def _(step):
        pl.semaphore_signal(
            barrier,
            inc=1,
            device_id={"serve": lax.rem(serve + step, serve_count)},
            device_id_type=MESH,
        )

    def target(step):
        return lax.rem(serve + step + 1, serve_count)

    def origin(step):
        return lax.rem(serve + 2 * serve_count - step - 1, serve_count)

    def token_start(group, place):
        return pl.multiple_of((group * serve_count + place) * rows, rows)

    def load(at, index):
        step = at * batch + index
        start = token_start(step // serve_count, target(lax.rem(step, serve_count)))
        return pltpu.make_async_copy(
            prefill_ref.at[:, pl.ds(start, rows), :],
            tokens.at[lax.rem(at, 2), index],
            load_sem.at[lax.rem(at, 2), index],
        )

    def partial_copy(step):
        return pltpu.make_async_remote_copy(
            src_ref=partial.at[step],
            dst_ref=arrived_partial.at[step],
            send_sem=partial_send.at[step],
            recv_sem=partial_recv.at[step],
            device_id={"tensor": peer},
            device_id_type=MESH,
        )

    def spread_copy(group, step, place):
        return pltpu.make_async_remote_copy(
            src_ref=piece.at[group * serve_count + step],
            dst_ref=spread[group].at[place],
            send_sem=spread_send.at[group * serve_count + step],
            recv_sem=spread_recv.at[group * serve_count + place],
            device_id={"serve": target(step)},
            device_id_type=MESH,
        )

    def home_copy(group, step, place):
        return pltpu.make_async_remote_copy(
            src_ref=staged.at[group * serve_count + step],
            dst_ref=latents.at[tensor, :, pl.ds(token_start(group, place), rows), :],
            send_sem=home_send.at[group * serve_count + step],
            recv_sem=home_recv.at[group * serve_count + place],
            device_id={"serve": target(step)},
            device_id_type=MESH,
        )

    def share_copy(group, place):
        part = latents.at[tensor, :, pl.ds(token_start(group, place), rows), :]
        return pltpu.make_async_remote_copy(
            src_ref=part,
            dst_ref=part,
            send_sem=share_send.at[group * serve_count + place],
            recv_sem=share_recv.at[group * serve_count + place],
            device_id={"tensor": peer},
            device_id_type=MESH,
        )

    history = cached.shape[1]
    kv_count = query_ref.shape[1]
    score_scale = HEAD_DIM ** (-0.5)

    def write_keys(key_rows, value_rows, cosines, sines, place, count):
        key_block = jnp.dot(
            key_rows.reshape(slot_count * count, width),
            up_key_ref[...],
            preferred_element_type=jnp.float32,
        )
        value_block = jnp.dot(
            value_rows.reshape(slot_count * count, width),
            up_value_ref[...],
            preferred_element_type=jnp.float32,
        ).astype(jnp.bfloat16)
        for index in range(slot_count):
            values[index, pl.ds(place, count), :] = value_block[index * count : (index + 1) * count]
            for head in range(kv_count):
                block = key_block[
                    index * count : (index + 1) * count, head * HEAD_DIM : (head + 1) * HEAD_DIM
                ]
                turned = pltpu.roll(block, HEAD_DIM // 2, 1)
                keys[index, pl.ds(place, count), head * HEAD_DIM : (head + 1) * HEAD_DIM] = (
                    block * cosines[index] + turned * sines[index]
                ).astype(jnp.bfloat16)

    cache_count = history // batch_count

    def cache_rows(step):
        place = pl.multiple_of(step * cache_count, cache_count)
        block = cached[:, pl.ds(place, cache_count), :]
        cosine = cosine_ref[pl.ds(place, cache_count), :]
        sine = sine_ref[pl.ds(place, cache_count), :]
        write_keys(
            block[..., :width],
            block[..., width:],
            [cosine] * slot_count,
            [sine] * slot_count,
            place,
            cache_count,
        )

    def span_rows(start):
        cosine = cosine_ref[pl.ds(start, rows), :]
        sine = sine_ref[pl.ds(start, rows), :]
        cosines = []
        sines = []
        for index in range(slot_count):
            turn_cosine = turn_ref[0, index : index + 1, :]
            turn_sine = turn_ref[1, index : index + 1, :]
            cosines.append(turn_cosine * cosine - turn_sine * sine)
            sines.append(turn_sine * cosine + turn_cosine * sine)
        block = latents[:, :, pl.ds(start, rows), :]
        write_keys(block[0], block[1], cosines, sines, pl.multiple_of(history + start, rows), rows)

    def score(index, head, first, count):
        block = keys[index, first : first + count, head * HEAD_DIM : (head + 1) * HEAD_DIM]
        return (
            lax.dot_general(
                query_ref[index, head],
                block,
                (((1,), (1,)), ((), ())),
                preferred_element_type=jnp.float32,
            )
            * score_scale
        )

    cache_load = pltpu.make_async_copy(cache_ref, cached, cache_sem.at[0])
    cache_load.start()
    for index in range(batch):
        load(0, index).start()
    pl.semaphore_wait(barrier, serve_count)
    peer_columns = pl.ds(pl.multiple_of(peer * width, width), width)
    own_columns = pl.ds(pl.multiple_of(tensor * width, width), width)

    def project(at):
        for index in range(batch):
            load(at, index).wait()

        @pl.when(at + 1 < batch_count)
        def _():
            for index in range(batch):
                load(at + 1, index).start()

        block = tokens[lax.rem(at, 2)].reshape(batch * slot_count * rows, -1)
        steps = pl.ds(pl.multiple_of(at * batch, batch), batch)
        partial[steps] = (
            jnp.dot(block, down_ref[:, peer_columns], preferred_element_type=jnp.float32)
            .astype(jnp.bfloat16)
            .reshape(batch, slot_count * rows, width)
        )
        for index in range(batch):
            partial_copy(at * batch + index).start()
        own[steps] = jnp.dot(
            block, down_ref[:, own_columns], preferred_element_type=jnp.float32
        ).reshape(batch, slot_count * rows, width)

    def finish(group, step):
        whole_step = group * serve_count + step
        partial_copy(whole_step).wait_recv()
        latent = own[whole_step] + arrived_partial[whole_step].astype(jnp.float32)
        latent = latent.astype(jnp.bfloat16).reshape(slot_count, rows, width)

        @pl.when(step < serve_count - 1)
        def _():
            piece[whole_step] = latent
            spread_copy(group, step, serve).start()

        @pl.when(step == serve_count - 1)
        def _():
            spread[group][serve] = latent

    def send_home(group):
        @pl.loop(0, serve_count - 1)
        def _(step):
            spread_copy(group, step, origin(step)).wait_recv()

        @pl.loop(0, serve_count)
        def _(step):
            place = group * serve_count + step
            for index in range(slot_count):
                source = source_ref[target(step) * slot_count + index]
                staged[place, index] = spread[group][
                    source // slot_count, lax.rem(source, slot_count)
                ]

            @pl.when(step < serve_count - 1)
            def _():
                home_copy(group, step, serve).start()

            @pl.when(step == serve_count - 1)
            def _():
                latents[tensor, :, pl.ds(token_start(group, serve), rows), :] = staged[place]
                share_copy(group, serve).start()

    def share(group, step):
        @pl.when(step < serve_count - 1)
        def _():
            home_copy(group, step, origin(step)).wait_recv()
            share_copy(group, origin(step)).start()

    def take(group, step):
        share_copy(group, origin(step)).wait_recv()
        span_rows(token_start(group, origin(step)))

    cache_load.wait()

    @pl.loop(0, batch_count)
    def _(at):
        project(at)
        cache_rows(at)

        if group_count > 1:

            @pl.when(at == group_batches + 2)
            def _():
                send_home(0)

        for group in range(group_count):
            first = group * group_batches

            @pl.when((at > first) & (at <= first + group_batches))
            def _():
                for index in range(batch):
                    finish(group, (at - 1 - first) * batch + index)

    for index in range(batch):
        finish(group_count - 1, serve_count - batch + index)

    if group_count > 1:

        @pl.loop(0, serve_count)
        def _(step):
            share(0, step)

    send_home(group_count - 1)

    for index in range(slot_count):
        row = lax.broadcasted_iota(jnp.int32, (query_ref.shape[2], history), 1)
        live = row < length_ref[index]
        for head in range(kv_count):
            scores[index, head, :, :history] = jnp.where(
                live, score(index, head, 0, history), -jnp.inf
            )

    @pl.loop(0, serve_count)
    def _(step):
        share(group_count - 1, step)
        if group_count > 1:
            take(0, step)

    span_store = pltpu.make_async_copy(latents.at[tensor], span_out, store_sem.at[0])
    span_store.start()

    @pl.loop(0, serve_count)
    def _(step):
        take(group_count - 1, step)

    span_count = latents.shape[2]
    for index in range(slot_count):
        for head in range(kv_count):
            cache_scores = scores[index, head, :, :history]
            span_scores = score(index, head, history, span_count)
            highest = jnp.maximum(
                jnp.max(cache_scores, axis=-1, keepdims=True),
                jnp.max(span_scores, axis=-1, keepdims=True),
            )
            cache_weights = jnp.exp(cache_scores - highest)
            span_weights = jnp.exp(span_scores - highest)
            total = jnp.sum(cache_weights, axis=-1, keepdims=True) + jnp.sum(
                span_weights, axis=-1, keepdims=True
            )
            columns = slice(head * HEAD_DIM, (head + 1) * HEAD_DIM)
            mixed = jnp.dot(
                (cache_weights / total).astype(jnp.bfloat16),
                values[index, :history, columns],
                preferred_element_type=jnp.float32,
            ) + jnp.dot(
                (span_weights / total).astype(jnp.bfloat16),
                values[index, history:, columns],
                preferred_element_type=jnp.float32,
            )
            attn_ref[index, head] = mixed.astype(jnp.bfloat16)

    for group in range(group_count):

        @pl.loop(0, serve_count)
        def _(step):
            share_copy(group, step).wait_send()
            partial_copy(group * serve_count + step).wait_send()

            @pl.when(step < serve_count - 1)
            def _():
                spread_copy(group, step, serve).wait_send()
                home_copy(group, step, serve).wait_send()

    span_store.wait()


def tables(count):
    frequency = ROPE_BASE ** (-np.arange(HEAD_DIM // 2) / (HEAD_DIM // 2))
    angles = np.arange(count)[:, None] * frequency
    cosine = np.cos(angles)
    sine = np.sin(angles)
    return (
        jnp.asarray(np.concatenate([cosine, cosine], axis=1), jnp.float32),
        jnp.asarray(np.concatenate([-sine, sine], axis=1), jnp.float32),
    )


def hand_off(
    prefill, down_proj, source_of, hist_len, rotated, turn, up_key, up_value, cache_latent
):
    slot_count, span_count, feature_count = prefill.shape
    serve_count = lax.axis_size("serve")
    width = down_proj.shape[1] // lax.axis_size("tensor")
    group_count = 2 if span_count % (serve_count * 2 * LEAST_ROWS) == 0 else 1
    piece_count = group_count * serve_count
    rows = span_count // piece_count
    batch = max(1, min(serve_count // 2, MATMUL_ROWS // (slot_count * rows)))
    half = jax.ShapeDtypeStruct((slot_count, span_count, width), jnp.bfloat16)
    pieces = (piece_count, slot_count, rows, width)
    flat = (piece_count, slot_count * rows, width)
    history = cache_latent.shape[1]
    cosine, sine = tables(max(history, span_count))
    vmem = pl.BlockSpec(memory_space=pltpu.VMEM)
    smem = pl.BlockSpec(memory_space=pltpu.SMEM)
    hbm = pl.BlockSpec(memory_space=pl.ANY)
    each = pltpu.SemaphoreType.DMA((piece_count,))
    return pl.pallas_call(
        hand_off_kernel,
        out_shape=(half, jax.ShapeDtypeStruct(rotated.shape, jnp.bfloat16)),
        in_specs=[hbm, vmem, smem, smem, vmem, vmem, vmem, vmem, vmem, vmem, hbm],
        out_specs=(hbm, vmem),
        scratch_shapes=[
            pltpu.VMEM((2, batch, slot_count, rows, feature_count), jnp.bfloat16),
            pltpu.VMEM(flat, jnp.bfloat16),
            pltpu.VMEM(flat, jnp.bfloat16),
            pltpu.VMEM(flat, jnp.float32),
            pltpu.VMEM(pieces, jnp.bfloat16),
            [pltpu.VMEM((serve_count,) + pieces[1:], jnp.bfloat16)] * group_count,
            pltpu.VMEM(pieces, jnp.bfloat16),
            pltpu.VMEM((2,) + half.shape, jnp.bfloat16),
            pltpu.VMEM(cache_latent.shape, jnp.bfloat16),
            pltpu.VMEM((slot_count, history + span_count, up_key.shape[1]), jnp.bfloat16),
            pltpu.VMEM((slot_count, history + span_count, up_key.shape[1]), jnp.bfloat16),
            pltpu.VMEM(rotated.shape[:3] + (history,), jnp.float32),
            pltpu.SemaphoreType.DMA((2, batch)),
            each,
            each,
            each,
            each,
            each,
            each,
            each,
            each,
            pltpu.SemaphoreType.DMA((1,)),
            pltpu.SemaphoreType.DMA((1,)),
        ],
        compiler_params=pltpu.CompilerParams(
            collective_id=0, has_side_effects=True, vmem_limit_bytes=56 * 2**20
        ),
        cost_estimate=pl.CostEstimate(
            flops=4 * slot_count * span_count * feature_count * width,
            bytes_accessed=2 * slot_count * span_count * feature_count,
            transcendentals=0,
        ),
    )(
        prefill,
        down_proj,
        source_of,
        hist_len,
        rotated,
        turn,
        cosine,
        sine,
        up_key,
        up_value,
        cache_latent,
    )


def shards(prefill, down_proj, up_key, up_value, queries, cache_latent, hist_len, assign):
    slot_count, span_count, _ = prefill.shape
    rank_width = down_proj.shape[1] // 2
    request = jnp.arange(assign.shape[0], dtype=jnp.int32)
    source_of = jnp.sum(jnp.where(assign[None, :] == request[:, None], request[None, :], 0), axis=1)
    kv_local = up_key.shape[1] // HEAD_DIM
    head_local = queries.shape[2] // HEAD_DIM
    group_size = head_local // kv_local
    step_count = queries.shape[1]
    query_pos = hist_len[:, None] + span_count + jnp.arange(step_count, dtype=jnp.int32)[None, :]
    rotated = rotate(
        queries.astype(jnp.float32).reshape(slot_count, step_count, head_local, HEAD_DIM), query_pos
    ).astype(jnp.bfloat16)
    rotated = jnp.swapaxes(
        rotated.reshape(slot_count, step_count, kv_local, group_size, HEAD_DIM), 1, 2
    ).reshape(slot_count, kv_local, step_count * group_size, HEAD_DIM)
    half = HEAD_DIM // 2
    frequency = ROPE_BASE ** (-jnp.arange(half, dtype=jnp.float32) / half)
    angles = hist_len.astype(jnp.float32)[:, None] * frequency
    cosine = jnp.cos(angles)
    sine = jnp.sin(angles)
    turn = jnp.stack(
        [jnp.concatenate([cosine, cosine], axis=1), jnp.concatenate([-sine, sine], axis=1)]
    )
    span_out, attn = hand_off(
        prefill, down_proj, source_of, hist_len, rotated, turn, up_key, up_value, cache_latent
    )
    attn = jnp.swapaxes(
        attn.reshape(slot_count, kv_local, step_count, group_size, HEAD_DIM), 1, 2
    ).reshape(slot_count, step_count, head_local * HEAD_DIM)
    return (attn, span_out)


def solution(mesh):
    return jax.shard_map(
        shards,
        mesh=mesh,
        in_specs=(
            P("serve", None, "tensor"),
            P("tensor", None),
            P(None, "tensor"),
            P(None, "tensor"),
            P("serve", None, "tensor"),
            P("serve", None, None),
            P("serve"),
            P(),
        ),
        out_specs=(P("serve", None, "tensor"), P("serve", None, "tensor")),
        check_vma=False,
    )
```

```python
import jax
import jax.numpy as jnp
import numpy as np
from jax import lax
from jax.experimental import pallas as pl
from jax.experimental.pallas import tpu as pltpu
from jax.sharding import PartitionSpec as P

HEAD_DIM = 128


ROPE_BASE = 500000.0


def rotate(vectors, positions):
    half = vectors.shape[-1] // 2
    frequency = ROPE_BASE ** (-jnp.arange(half, dtype=jnp.float32) / half)
    angles = positions.astype(jnp.float32)[..., None, None] * frequency
    cosine = jnp.cos(angles)
    sine = jnp.sin(angles)
    first_half = vectors[..., :half]
    second_half = vectors[..., half:]
    return jnp.concatenate(
        [first_half * cosine - second_half * sine, second_half * cosine + first_half * sine],
        axis=-1,
    )


MESH = pl.DeviceIdType.MESH
MATMUL_ROWS = 256
LEAST_ROWS = 16


def hand_off_kernel(
    prefill_ref,
    down_ref,
    source_ref,
    length_ref,
    query_ref,
    turn_ref,
    cosine_ref,
    sine_ref,
    up_key_ref,
    up_value_ref,
    cache_ref,
    span_out,
    attn_ref,
    tokens,
    partial,
    arrived_partial,
    own,
    piece,
    spread,
    staged,
    latents,
    cached,
    keys,
    values,
    scores,
    load_sem,
    partial_send,
    partial_recv,
    spread_send,
    spread_recv,
    home_send,
    home_recv,
    share_send,
    share_recv,
    store_sem,
    cache_sem,
):
    group_count = len(spread)
    serve_count, slot_count, rows, width = spread[0].shape
    piece_count = group_count * serve_count
    batch = tokens.shape[1]
    batch_count = piece_count // batch
    group_batches = serve_count // batch
    tensor = lax.axis_index("tensor")
    serve = lax.axis_index("serve")
    peer = 1 - tensor

    barrier = pltpu.get_barrier_semaphore()
    pl.semaphore_signal(barrier, inc=1, device_id={"tensor": peer}, device_id_type=MESH)

    @pl.loop(1, serve_count)
    def _(step):
        pl.semaphore_signal(
            barrier,
            inc=1,
            device_id={"serve": lax.rem(serve + step, serve_count)},
            device_id_type=MESH,
        )

    def target(step):
        return lax.rem(serve + step + 1, serve_count)

    def origin(step):
        return lax.rem(serve + 2 * serve_count - step - 1, serve_count)

    def token_start(group, place):
        return pl.multiple_of((group * serve_count + place) * rows, rows)

    def load(at, index):
        step = at * batch + index
        start = token_start(step // serve_count, target(lax.rem(step, serve_count)))
        return pltpu.make_async_copy(
            prefill_ref.at[:, pl.ds(start, rows), :],
            tokens.at[lax.rem(at, 2), index],
            load_sem.at[lax.rem(at, 2), index],
        )

    def partial_copy(step):
        return pltpu.make_async_remote_copy(
            src_ref=partial.at[step],
            dst_ref=arrived_partial.at[step],
            send_sem=partial_send.at[step],
            recv_sem=partial_recv.at[step],
            device_id={"tensor": peer},
            device_id_type=MESH,
        )

    def spread_copy(group, step, place):
        return pltpu.make_async_remote_copy(
            src_ref=piece.at[group * serve_count + step],
            dst_ref=spread[group].at[place],
            send_sem=spread_send.at[group * serve_count + step],
            recv_sem=spread_recv.at[group * serve_count + place],
            device_id={"serve": target(step)},
            device_id_type=MESH,
        )

    def home_copy(group, step, place):
        return pltpu.make_async_remote_copy(
            src_ref=staged.at[group * serve_count + step],
            dst_ref=latents.at[tensor, :, pl.ds(token_start(group, place), rows), :],
            send_sem=home_send.at[group * serve_count + step],
            recv_sem=home_recv.at[group * serve_count + place],
            device_id={"serve": target(step)},
            device_id_type=MESH,
        )

    def share_copy(group, place):
        part = latents.at[tensor, :, pl.ds(token_start(group, place), rows), :]
        return pltpu.make_async_remote_copy(
            src_ref=part,
            dst_ref=part,
            send_sem=share_send.at[group * serve_count + place],
            recv_sem=share_recv.at[group * serve_count + place],
            device_id={"tensor": peer},
            device_id_type=MESH,
        )

    history = cached.shape[1]
    kv_count = query_ref.shape[1]
    score_scale = HEAD_DIM ** (-0.5)

    def write_keys(key_rows, value_rows, cosines, sines, place, count):
        key_block = jnp.dot(
            key_rows.reshape(slot_count * count, width),
            up_key_ref[...],
            preferred_element_type=jnp.float32,
        )
        value_block = jnp.dot(
            value_rows.reshape(slot_count * count, width),
            up_value_ref[...],
            preferred_element_type=jnp.float32,
        ).astype(jnp.bfloat16)
        for index in range(slot_count):
            values[index, pl.ds(place, count), :] = value_block[index * count : (index + 1) * count]
            for head in range(kv_count):
                block = key_block[
                    index * count : (index + 1) * count, head * HEAD_DIM : (head + 1) * HEAD_DIM
                ]
                turned = pltpu.roll(block, HEAD_DIM // 2, 1)
                keys[index, pl.ds(place, count), head * HEAD_DIM : (head + 1) * HEAD_DIM] = (
                    block * cosines[index] + turned * sines[index]
                ).astype(jnp.bfloat16)

    cache_count = history // batch_count

    def cache_rows(step):
        place = pl.multiple_of(step * cache_count, cache_count)
        block = cached[:, pl.ds(place, cache_count), :]
        cosine = cosine_ref[pl.ds(place, cache_count), :]
        sine = sine_ref[pl.ds(place, cache_count), :]
        write_keys(
            block[..., :width],
            block[..., width:],
            [cosine] * slot_count,
            [sine] * slot_count,
            place,
            cache_count,
        )

    def span_rows(start):
        cosine = cosine_ref[pl.ds(start, rows), :]
        sine = sine_ref[pl.ds(start, rows), :]
        cosines = []
        sines = []
        for index in range(slot_count):
            turn_cosine = turn_ref[0, index : index + 1, :]
            turn_sine = turn_ref[1, index : index + 1, :]
            cosines.append(turn_cosine * cosine - turn_sine * sine)
            sines.append(turn_sine * cosine + turn_cosine * sine)
        block = latents[:, :, pl.ds(start, rows), :]
        write_keys(block[0], block[1], cosines, sines, pl.multiple_of(history + start, rows), rows)

    def score(index, head, first, count):
        block = keys[index, first : first + count, head * HEAD_DIM : (head + 1) * HEAD_DIM]
        return (
            lax.dot_general(
                query_ref[index, head],
                block,
                (((1,), (1,)), ((), ())),
                preferred_element_type=jnp.float32,
            )
            * score_scale
        )

    cache_load = pltpu.make_async_copy(cache_ref, cached, cache_sem.at[0])
    cache_load.start()
    for index in range(batch):
        load(0, index).start()
    pl.semaphore_wait(barrier, serve_count)
    peer_columns = pl.ds(pl.multiple_of(peer * width, width), width)
    own_columns = pl.ds(pl.multiple_of(tensor * width, width), width)

    def project(at):
        for index in range(batch):
            load(at, index).wait()

        @pl.when(at + 1 < batch_count)
        def _():
            for index in range(batch):
                load(at + 1, index).start()

        block = tokens[lax.rem(at, 2)].reshape(batch * slot_count * rows, -1)
        steps = pl.ds(pl.multiple_of(at * batch, batch), batch)
        partial[steps] = (
            jnp.dot(block, down_ref[:, peer_columns], preferred_element_type=jnp.float32)
            .astype(jnp.bfloat16)
            .reshape(batch, slot_count * rows, width)
        )
        for index in range(batch):
            partial_copy(at * batch + index).start()
        own[steps] = jnp.dot(
            block, down_ref[:, own_columns], preferred_element_type=jnp.float32
        ).reshape(batch, slot_count * rows, width)

    def finish(group, step):
        whole_step = group * serve_count + step
        partial_copy(whole_step).wait_recv()
        latent = own[whole_step] + arrived_partial[whole_step].astype(jnp.float32)
        latent = latent.astype(jnp.bfloat16).reshape(slot_count, rows, width)

        @pl.when(step < serve_count - 1)
        def _():
            piece[whole_step] = latent
            spread_copy(group, step, serve).start()

        @pl.when(step == serve_count - 1)
        def _():
            spread[group][serve] = latent

    def send_home(group):
        @pl.loop(0, serve_count - 1)
        def _(step):
            spread_copy(group, step, origin(step)).wait_recv()

        @pl.loop(0, serve_count)
        def _(step):
            place = group * serve_count + step
            for index in range(slot_count):
                source = source_ref[target(step) * slot_count + index]
                staged[place, index] = spread[group][
                    source // slot_count, lax.rem(source, slot_count)
                ]

            @pl.when(step < serve_count - 1)
            def _():
                home_copy(group, step, serve).start()

            @pl.when(step == serve_count - 1)
            def _():
                latents[tensor, :, pl.ds(token_start(group, serve), rows), :] = staged[place]
                share_copy(group, serve).start()

    def share(group, step):
        @pl.when(step < serve_count - 1)
        def _():
            home_copy(group, step, origin(step)).wait_recv()
            share_copy(group, origin(step)).start()

    def take(group, step):
        share_copy(group, origin(step)).wait_recv()
        span_rows(token_start(group, origin(step)))

    cache_load.wait()

    @pl.loop(0, batch_count)
    def _(at):
        project(at)
        cache_rows(at)

        if group_count > 1:

            @pl.when(at == group_batches + 1)
            def _():
                send_home(0)

        for group in range(group_count):
            first = group * group_batches

            @pl.when((at > first) & (at <= first + group_batches))
            def _():
                for index in range(batch):
                    finish(group, (at - 1 - first) * batch + index)

    for index in range(batch):
        finish(group_count - 1, serve_count - batch + index)

    if group_count > 1:

        @pl.loop(0, serve_count)
        def _(step):
            share(0, step)

    send_home(group_count - 1)

    for index in range(slot_count):
        row = lax.broadcasted_iota(jnp.int32, (query_ref.shape[2], history), 1)
        live = row < length_ref[index]
        for head in range(kv_count):
            scores[index, head, :, :history] = jnp.where(
                live, score(index, head, 0, history), -jnp.inf
            )

    @pl.loop(0, serve_count)
    def _(step):
        share(group_count - 1, step)
        if group_count > 1:
            take(0, step)

    span_store = pltpu.make_async_copy(latents.at[tensor], span_out, store_sem.at[0])
    span_store.start()

    early = history + (group_count - 1) * serve_count * rows
    if group_count > 1:
        for index in range(slot_count):
            for head in range(kv_count):
                scores[index, head, :, history:] = score(index, head, history, early - history)

    @pl.loop(0, serve_count)
    def _(step):
        take(group_count - 1, step)

    span_count = latents.shape[2]
    for index in range(slot_count):
        for head in range(kv_count):
            cache_scores = scores[index, head]
            span_scores = score(index, head, early, history + span_count - early)
            highest = jnp.maximum(
                jnp.max(cache_scores, axis=-1, keepdims=True),
                jnp.max(span_scores, axis=-1, keepdims=True),
            )
            cache_weights = jnp.exp(cache_scores - highest)
            span_weights = jnp.exp(span_scores - highest)
            total = jnp.sum(cache_weights, axis=-1, keepdims=True) + jnp.sum(
                span_weights, axis=-1, keepdims=True
            )
            columns = slice(head * HEAD_DIM, (head + 1) * HEAD_DIM)
            mixed = jnp.dot(
                (cache_weights / total).astype(jnp.bfloat16),
                values[index, :early, columns],
                preferred_element_type=jnp.float32,
            ) + jnp.dot(
                (span_weights / total).astype(jnp.bfloat16),
                values[index, early:, columns],
                preferred_element_type=jnp.float32,
            )
            attn_ref[index, head] = mixed.astype(jnp.bfloat16)

    for group in range(group_count):

        @pl.loop(0, serve_count)
        def _(step):
            share_copy(group, step).wait_send()
            partial_copy(group * serve_count + step).wait_send()

            @pl.when(step < serve_count - 1)
            def _():
                spread_copy(group, step, serve).wait_send()
                home_copy(group, step, serve).wait_send()

    span_store.wait()


def tables(count):
    frequency = ROPE_BASE ** (-np.arange(HEAD_DIM // 2) / (HEAD_DIM // 2))
    angles = np.arange(count)[:, None] * frequency
    cosine = np.cos(angles)
    sine = np.sin(angles)
    return (
        jnp.asarray(np.concatenate([cosine, cosine], axis=1), jnp.float32),
        jnp.asarray(np.concatenate([-sine, sine], axis=1), jnp.float32),
    )


def hand_off(
    prefill, down_proj, source_of, hist_len, rotated, turn, up_key, up_value, cache_latent
):
    slot_count, span_count, feature_count = prefill.shape
    serve_count = lax.axis_size("serve")
    width = down_proj.shape[1] // lax.axis_size("tensor")
    group_count = 2 if span_count % (serve_count * 2 * LEAST_ROWS) == 0 else 1
    piece_count = group_count * serve_count
    rows = span_count // piece_count
    batch = max(1, min(serve_count // 2, MATMUL_ROWS // (slot_count * rows)))
    half = jax.ShapeDtypeStruct((slot_count, span_count, width), jnp.bfloat16)
    pieces = (piece_count, slot_count, rows, width)
    flat = (piece_count, slot_count * rows, width)
    history = cache_latent.shape[1]
    cosine, sine = tables(max(history, span_count))
    vmem = pl.BlockSpec(memory_space=pltpu.VMEM)
    smem = pl.BlockSpec(memory_space=pltpu.SMEM)
    hbm = pl.BlockSpec(memory_space=pl.ANY)
    each = pltpu.SemaphoreType.DMA((piece_count,))
    return pl.pallas_call(
        hand_off_kernel,
        out_shape=(half, jax.ShapeDtypeStruct(rotated.shape, jnp.bfloat16)),
        in_specs=[hbm, vmem, smem, smem, vmem, vmem, vmem, vmem, vmem, vmem, hbm],
        out_specs=(hbm, vmem),
        scratch_shapes=[
            pltpu.VMEM((2, batch, slot_count, rows, feature_count), jnp.bfloat16),
            pltpu.VMEM(flat, jnp.bfloat16),
            pltpu.VMEM(flat, jnp.bfloat16),
            pltpu.VMEM(flat, jnp.float32),
            pltpu.VMEM(pieces, jnp.bfloat16),
            [pltpu.VMEM((serve_count,) + pieces[1:], jnp.bfloat16)] * group_count,
            pltpu.VMEM(pieces, jnp.bfloat16),
            pltpu.VMEM((2,) + half.shape, jnp.bfloat16),
            pltpu.VMEM(cache_latent.shape, jnp.bfloat16),
            pltpu.VMEM((slot_count, history + span_count, up_key.shape[1]), jnp.bfloat16),
            pltpu.VMEM((slot_count, history + span_count, up_key.shape[1]), jnp.bfloat16),
            pltpu.VMEM(
                rotated.shape[:3] + (history + (group_count - 1) * serve_count * rows,), jnp.float32
            ),
            pltpu.SemaphoreType.DMA((2, batch)),
            each,
            each,
            each,
            each,
            each,
            each,
            each,
            each,
            pltpu.SemaphoreType.DMA((1,)),
            pltpu.SemaphoreType.DMA((1,)),
        ],
        compiler_params=pltpu.CompilerParams(
            collective_id=0, has_side_effects=True, vmem_limit_bytes=56 * 2**20
        ),
        cost_estimate=pl.CostEstimate(
            flops=4 * slot_count * span_count * feature_count * width,
            bytes_accessed=2 * slot_count * span_count * feature_count,
            transcendentals=0,
        ),
    )(
        prefill,
        down_proj,
        source_of,
        hist_len,
        rotated,
        turn,
        cosine,
        sine,
        up_key,
        up_value,
        cache_latent,
    )


def shards(prefill, down_proj, up_key, up_value, queries, cache_latent, hist_len, assign):
    slot_count, span_count, _ = prefill.shape
    rank_width = down_proj.shape[1] // 2
    request = jnp.arange(assign.shape[0], dtype=jnp.int32)
    source_of = jnp.sum(jnp.where(assign[None, :] == request[:, None], request[None, :], 0), axis=1)
    kv_local = up_key.shape[1] // HEAD_DIM
    head_local = queries.shape[2] // HEAD_DIM
    group_size = head_local // kv_local
    step_count = queries.shape[1]
    query_pos = hist_len[:, None] + span_count + jnp.arange(step_count, dtype=jnp.int32)[None, :]
    rotated = rotate(
        queries.astype(jnp.float32).reshape(slot_count, step_count, head_local, HEAD_DIM), query_pos
    ).astype(jnp.bfloat16)
    rotated = jnp.swapaxes(
        rotated.reshape(slot_count, step_count, kv_local, group_size, HEAD_DIM), 1, 2
    ).reshape(slot_count, kv_local, step_count * group_size, HEAD_DIM)
    half = HEAD_DIM // 2
    frequency = ROPE_BASE ** (-jnp.arange(half, dtype=jnp.float32) / half)
    angles = hist_len.astype(jnp.float32)[:, None] * frequency
    cosine = jnp.cos(angles)
    sine = jnp.sin(angles)
    turn = jnp.stack(
        [jnp.concatenate([cosine, cosine], axis=1), jnp.concatenate([-sine, sine], axis=1)]
    )
    span_out, attn = hand_off(
        prefill, down_proj, source_of, hist_len, rotated, turn, up_key, up_value, cache_latent
    )
    attn = jnp.swapaxes(
        attn.reshape(slot_count, kv_local, step_count, group_size, HEAD_DIM), 1, 2
    ).reshape(slot_count, step_count, head_local * HEAD_DIM)
    return (attn, span_out)


def solution(mesh):
    return jax.shard_map(
        shards,
        mesh=mesh,
        in_specs=(
            P("serve", None, "tensor"),
            P("tensor", None),
            P(None, "tensor"),
            P(None, "tensor"),
            P("serve", None, "tensor"),
            P("serve", None, None),
            P("serve"),
            P(),
        ),
        out_specs=(P("serve", None, "tensor"), P("serve", None, "tensor")),
        check_vma=False,
    )
```
